32 devices in a mesh: sec: 2 (over y), tube: 4 (over z), blk: 2 (over x), sub: 2 (over core).
Axes of the slice: x: 2, y: 2, z: 4, core: 2. Of those that a mesh axis runs over, the one named last changes fastest.
Arguments:
- latent: float32 [2048, 256], P(('sec', 'tube'), 'blk'), parts along dimension 0, may hold values from 0.2 to 5
- weight_maps: bfloat16 [8, 2048, 256], P('sub', ('sec', 'tube'), 'blk'), parts along dimension 1, may hold values from 0.039794922 to 0.19921875
- row_taps: float32 [8, 31], P('sub'), may hold values from 0.05 to 1
- col_taps: float32 [8, 31], P('sub'), may hold values from 0.05 to 1
- exposures: bfloat16 [2, 512, 128, 128], P('blk', ('sec', 'tube')), parts along dimension 1, may hold values from 0.19921875 to 5
- gains: bfloat16 [2, 512], P('blk', ('sec', 'tube')), parts along dimension 1, may hold values from 0.5 to 2
- owners: int32 [2, 512, 1], P('blk', ('sec', 'tube')), parts along dimension 1, may hold values from 0 to 3, as said below
- offsets: int32 [2, 512], P('blk', ('sec', 'tube')), parts along dimension 1, may hold values from 0 to 1, as said below
Outputs:
- updated: float32 [2048, 256], P(('sec', 'tube'), 'blk'), parts along dimension 0
The draws below stay inside these ranges and needn't reach their ends.
There are 2 independent parts, one for each index of `sec`. The reference program is written for one: setup_inputs(seed, part) draws one part's arguments, and reference() takes and returns one part's arrays. A program takes and returns all parts, laid end to end along the dimension named above; an argument that names none is the same for every part. Nothing has to cross between parts.
Inputs may be any that keep to these rules, and one draw needn't show every extreme that they name: `owners`: among the 64 slots of one device no tube position is named more than 32 times; in each column of blocks some tube position is named exactly 32 times by every device of that column. `offsets`: some block places of the image receive no slot.
All inputs are finite; a program needn't handle non-finite values.
Results may differ from the reference program's by a relative error of at most 0.00035.
Values may be sent and summed in bfloat16 or wider, within the bound.
A program may use at most 64 MiB of HBM per device.

```python
import math
import jax
import jax.numpy as jnp

KB = 8
TAPS = 31
BLOCK = 128
SLOTS = 64
ROW_BLOCKS = 2
ROWS = 1024
COLS = 256
CAP = 32
N_TUBE = 4
N_BLK = 2


def route_plan(key):
    folded = jax.random.fold_in(key, 41)
    subkeys = jax.random.split(folded, 8)
    active_tube = jax.random.randint(subkeys[0], (N_BLK, 1, 1), 0, N_TUBE)
    favour = jax.random.randint(subkeys[1], (N_BLK, 1, N_TUBE), 0, 4)
    jitter = jax.random.randint(subkeys[2], (N_BLK, N_TUBE, N_TUBE), 0, 4096)
    positions = jnp.arange(N_TUBE, dtype=jnp.int32)[None, None, :]
    scores = jnp.where(positions == active_tube, -1, (favour * 4096 + jitter) * N_TUBE + positions)
    ranking = jnp.argsort(-scores, axis=2)
    slot_index = jnp.arange(SLOTS, dtype=jnp.int32)
    cycle_index = jnp.maximum(slot_index - CAP, 0) % (N_TUBE - 1)
    cycle_index = jnp.broadcast_to(cycle_index[None, None, :], (N_BLK, N_TUBE, SLOTS))
    chosen_tube = jnp.take_along_axis(ranking, cycle_index, axis=2)
    unshuffled = jnp.where(slot_index[None, None, :] < CAP, active_tube, chosen_tube)
    shuffle_scores = jax.random.randint(subkeys[3], (N_BLK, N_TUBE, SLOTS), 0, 65536) * SLOTS + slot_index[None, None, :]
    shuffled = jnp.argsort(shuffle_scores, axis=2)
    owner_plan = jnp.take_along_axis(unshuffled, shuffled, axis=2).reshape(N_BLK, N_TUBE * SLOTS)
    dead_tube = jax.random.randint(subkeys[4], (N_BLK, 1), 0, N_TUBE)
    dead_row = jax.random.randint(subkeys[5], (N_BLK, 1), 0, ROW_BLOCKS)
    free_rows = jax.random.randint(subkeys[6], (N_BLK, N_TUBE * SLOTS), 0, ROW_BLOCKS)
    neighbour_rows = jax.random.randint(subkeys[7], (N_BLK, N_TUBE * SLOTS), 0, ROW_BLOCKS - 1)
    neighbour_rows = neighbour_rows + (neighbour_rows >= dead_row).astype(neighbour_rows.dtype)
    offset_plan = jnp.where(owner_plan == dead_tube, neighbour_rows, free_rows)
    return (owner_plan.astype(jnp.int32), offset_plan.astype(jnp.int32))


def draw_owners(key, part):
    return route_plan(key)[0][:, :, None]


def draw_offsets(key, part):
    return route_plan(key)[1]


def level_of(own_key, dims, cuts, least, high):
    gain = 1.0
    for dim, blocks in cuts:
        draws = jax.random.uniform(jax.random.fold_in(jax.random.fold_in(own_key, 6), dim), (blocks,), jnp.float32, least / len(cuts), high / len(cuts))
        gain = gain * jnp.repeat(jnp.exp(draws), dims[dim] // blocks).reshape((-1,) + (1,) * (len(dims) - 1 - dim))
    return gain


def setup_inputs(seed: int = 0, part: int = 0) -> dict:
    arg_keys = jax.random.split(jax.random.key(seed), 9)
    own_keys = jax.random.split(jax.random.fold_in(arg_keys[8], part), 9)
    return {
        "latent": jnp.clip(jnp.exp(math.log(5.0) - 3.218876 * jax.random.uniform(own_keys[0], (ROWS, COLS), jnp.float32) ** level_of(own_keys[0], (ROWS, COLS), ((0, 4), (1, 2)), -0.2, 0.2)), 0.2, 5.0),
        "weight_maps": jnp.clip(jnp.exp(math.log(0.19921875) - 1.61066415 * jax.random.uniform(own_keys[1], (KB, ROWS, COLS), jnp.float32) ** level_of(own_keys[1], (KB, ROWS, COLS), ((0, 2), (1, 4), (2, 2)), -0.2, 0.2)), 0.039794922, 0.19921875).astype(jnp.bfloat16),
        "row_taps": jnp.clip(jnp.exp(math.log(1.0) - 2.9957323 * jax.random.uniform(arg_keys[2], (KB, TAPS), jnp.float32) ** level_of(arg_keys[2], (KB, TAPS), ((0, 2),), -0.2, 0.2)), 0.05, 1.0),
        "col_taps": jnp.clip(jnp.exp(math.log(1.0) - 2.9957323 * jax.random.uniform(arg_keys[3], (KB, TAPS), jnp.float32) ** level_of(arg_keys[3], (KB, TAPS), ((0, 2),), -0.2, 0.2)), 0.05, 1.0),
        "exposures": jnp.clip(jnp.exp(math.log(5.0) - 3.2227897 * jax.random.uniform(own_keys[4], (N_BLK, N_TUBE * SLOTS, BLOCK, BLOCK), jnp.float32) ** level_of(own_keys[4], (N_BLK, N_TUBE * SLOTS, BLOCK, BLOCK), ((0, 2), (1, 4)), -0.2, 0.2)), 0.19921875, 5.0).astype(jnp.bfloat16),
        "gains": jnp.clip(jnp.exp(math.log(2.0) - 1.3862944 * jax.random.uniform(own_keys[5], (N_BLK, N_TUBE * SLOTS), jnp.float32) ** level_of(own_keys[5], (N_BLK, N_TUBE * SLOTS), ((0, 2), (1, 4)), -0.2, 0.2)), 0.5, 2.0).astype(jnp.bfloat16),
        "owners": draw_owners(jax.random.fold_in(jax.random.fold_in(arg_keys[8], part), 71), part),
        "offsets": draw_offsets(jax.random.fold_in(jax.random.fold_in(arg_keys[8], part), 71), part),
    }


def blur_field(field, row_weights, col_weights):
    margin = TAPS // 2
    padded = jnp.pad(field, ((margin, margin), (0, 0)))
    padded = jnp.concatenate([padded[:, -margin:], padded, padded[:, :margin]], axis=1)
    row_pass = row_weights[0] * padded[0:ROWS, :]
    for tap_index in range(1, TAPS):
        row_pass = row_pass + row_weights[tap_index] * padded[tap_index:tap_index + ROWS, :]
    step_output = col_weights[0] * row_pass[:, 0:COLS]
    for tap_index in range(1, TAPS):
        step_output = step_output + col_weights[tap_index] * row_pass[:, tap_index:tap_index + COLS]
    return step_output


def reference(latent, weight_maps, row_taps, col_taps, exposures, gains, owners, offsets):
    row_norm = row_taps / jnp.sum(row_taps, axis=1, keepdims=True)
    col_norm = col_taps / jnp.sum(col_taps, axis=1, keepdims=True)
    weight_stack = weight_maps.astype(jnp.float32)
    smeared_image = jnp.zeros((ROWS, COLS), jnp.float32)
    for kernel in range(KB):
        smeared_image = smeared_image + weight_stack[kernel] * blur_field(latent, row_norm[kernel], col_norm[kernel])
    block_rows = (owners[:, :, 0] * ROW_BLOCKS + offsets).astype(jnp.int32)
    block_cols = jnp.broadcast_to(jnp.arange(N_BLK, dtype=jnp.int32)[:, None], block_rows.shape)
    count_blocks = jnp.zeros((N_BLK, N_TUBE * ROW_BLOCKS, BLOCK, BLOCK), jnp.float32)
    count_blocks = count_blocks.at[block_cols, block_rows].add(exposures.astype(jnp.float32))
    gain_blocks = jnp.zeros((N_BLK, N_TUBE * ROW_BLOCKS), jnp.float32)
    gain_blocks = gain_blocks.at[block_cols, block_rows].add(gains.astype(jnp.float32))
    counts = jnp.transpose(count_blocks, (1, 2, 0, 3)).reshape(ROWS, COLS)
    coverage = jnp.repeat(jnp.repeat(gain_blocks.T, BLOCK, axis=0), BLOCK, axis=1)
    quotient = counts / smeared_image
    numerator = jnp.zeros((ROWS, COLS), jnp.float32)
    denominator = jnp.zeros((ROWS, COLS), jnp.float32)
    for kernel in range(KB):
        flip_rows = row_norm[kernel][::-1]
        flip_cols = col_norm[kernel][::-1]
        numerator = numerator + blur_field(weight_stack[kernel] * quotient, flip_rows, flip_cols)
        denominator = denominator + blur_field(weight_stack[kernel] * coverage, flip_rows, flip_cols)
    return latent * numerator / jnp.maximum(denominator, 0.25)
```

```python
import functools

import jax
import jax.numpy as jnp
from jax import lax
from jax.experimental import pallas as pl
from jax.experimental.pallas import tpu as pltpu
from jax.sharding import PartitionSpec as P

MESH = pl.DeviceIdType.MESH
F32 = jnp.float32
BF16 = jnp.bfloat16
HALO = 16
PACK = 3
CHUNK = 8


def dot(a, b):
    return jnp.dot(a, b, preferred_element_type=F32)


def band(base, shift, rows):
    wide = jnp.broadcast_to(base, (rows, base.shape[1]))
    return pltpu.roll(wide, shift, 1, stride=1, stride_axis=0)


def kernel(
    tubes,
    blks,
    latent_ref,
    weight_ref,
    row_ref,
    col_ref,
    exposure_ref,
    gain_ref,
    owner_ref,
    offset_ref,
    out_ref,
    exposure_buf,
    latent_half,
    view,
    side_view,
    weight_other,
    tap_own,
    tap_other,
    gain_send,
    gain_recv,
    mask,
    count_send,
    count_recv,
    row_band,
    row_band_t,
    col_band,
    scaled,
    spread,
    main_send,
    strip_send,
    packed_send,
    main_recv,
    edge_recv,
    packed_recv,
    corner_recv,
    total,
    load_sem,
    view_send,
    view_recv,
    weight_sem,
    tap_sem,
    gain_ssem,
    gain_rsem,
    count_ssem,
    count_rsem,
    field_ssem,
    main_rsem,
    edge_rsem,
    packed_rsem,
    corner_rsem,
):
    rows, block = latent_ref.shape
    half = rows // 2
    ext = half + 2 * HALO
    inner = half + HALO
    group = inner // PACK
    kernels = weight_ref.shape[0]
    taps = row_ref.shape[1]
    margin = taps // 2
    slots = exposure_ref.shape[0]
    t = lax.axis_index("tube")
    b = lax.axis_index("blk")
    s = lax.axis_index("sub")
    o = 1 - s
    sides = (1,) if blks == 2 else (1, -1)
    ahead = t + 1 - 2 * s
    behind = t - 1 + 2 * s
    has_ahead = (ahead >= 0) & (ahead < tubes)
    has_behind = (behind >= 0) & (behind < tubes)

    def blk_at(step):
        return lax.rem(b + step + blks, blks)

    def at(tube=None, blk=None, sub=None):
        return {
            "tube": t if tube is None else tube,
            "blk": b if blk is None else blk,
            "sub": s if sub is None else sub,
        }

    def remote(src, dst, ssem, rsem, device):
        return pltpu.make_async_remote_copy(
            src_ref=src,
            dst_ref=dst,
            send_sem=ssem,
            recv_sem=rsem,
            device_id=device,
            device_id_type=MESH,
        )

    loads = [
        pltpu.make_async_copy(
            exposure_ref.at[pl.ds(c * CHUNK, CHUNK)],
            exposure_buf.at[pl.ds(c * CHUNK, CHUNK)],
            load_sem.at[c],
        )
        for c in range(slots // CHUNK)
    ]
    for load in loads:
        load.start()

    barrier = pltpu.get_barrier_semaphore()
    near = [0] + list(sides)
    fixed = 0
    for step in near:
        for sub in (s, o):
            if step == 0 and sub is s:
                continue
            pl.semaphore_signal(barrier, inc=1, device_id=at(blk=blk_at(step), sub=sub), device_id_type=MESH)
            fixed += 1
    for j in range(1, tubes):
        pl.semaphore_signal(
            barrier, inc=1, device_id=at(tube=lax.rem(t + j, tubes)), device_id_type=MESH
        )
        fixed += 1
    extra = 2 * len(near) - 1
    for beside in (t - 1, t + 1):

        @pl.when((beside >= 0) & (beside < tubes))
        def _():
            for step in near:
                for sub in (s, o):
                    if step == 0 and sub is s:
                        continue
                    pl.semaphore_signal(
                        barrier,
                        inc=1,
                        device_id=at(tube=beside, blk=blk_at(step), sub=sub),
                        device_id_type=MESH,
                    )

    latent_half[...] = latent_ref[...].astype(BF16)
    tap_own[...] = jnp.zeros_like(tap_own)
    tap_own[0:kernels, 0:taps] = row_ref[...]
    tap_own[kernels : 2 * kernels, 0:taps] = col_ref[...]
    eye = lax.broadcasted_iota(jnp.int32, (slots, slots), 0) == lax.broadcasted_iota(
        jnp.int32, (slots, slots), 1
    )
    offset = jnp.sum(
        jnp.where(eye, jnp.broadcast_to(offset_ref[...].astype(F32), (slots, slots)), 0.0),
        axis=1,
        keepdims=True,
    )
    gain = jnp.sum(
        jnp.where(eye, jnp.broadcast_to(gain_ref[...].astype(F32), (slots, slots)), 0.0),
        axis=1,
        keepdims=True,
    )
    owner = owner_ref[...].astype(F32)
    here = s.astype(F32)
    for p in range(tubes):
        hit = jnp.where((owner == float(p)) & (offset == here), 1.0, 0.0)
        mask[p] = jnp.broadcast_to(hit, (slots, block))
        gain_send[p] = jnp.broadcast_to(jnp.sum(hit * gain, axis=0, keepdims=True), (8, block))

    pl.semaphore_wait(
        barrier,
        fixed + extra * ((t > 0).astype(jnp.int32) + (t < tubes - 1).astype(jnp.int32)),
    )

    tap_copy = remote(tap_own, tap_other, tap_sem.at[0], tap_sem.at[1], at(sub=o))
    tap_copy.start()
    weight_copy = remote(
        weight_ref.at[:, pl.ds(o * half, half)],
        weight_other,
        weight_sem.at[0],
        weight_sem.at[1],
        at(sub=o),
    )
    weight_copy.start()
    gain_copies = []
    for j in range(1, tubes):
        p = lax.rem(t + j, tubes)
        gain_copies.append(
            remote(gain_send.at[p], gain_recv.at[j - 1], gain_ssem.at[j - 1], gain_rsem.at[j - 1], at(tube=p))
        )
        gain_copies[-1].start()
    own_rows = pl.ds(pl.multiple_of(s * (rows - inner), HALO), inner)
    own_place = pl.ds(pl.multiple_of(o * HALO, HALO), inner)
    edge_rows = pl.ds(pl.multiple_of(o * (rows - HALO), HALO), HALO)
    edge_place = pl.ds(pl.multiple_of(s * inner, HALO), HALO)
    edge_copies = [
        remote(
            latent_half.at[edge_rows],
            view.at[edge_place],
            view_send.at[0],
            view_recv.at[0],
            at(tube=ahead),
        )
    ]
    side_copies = []
    for i, step in enumerate(sides):
        side_copies.append(
            remote(
                latent_half.at[own_rows],
                side_view.at[i, own_place],
                view_send.at[1 + 2 * i],
                view_recv.at[1 + 2 * i],
                at(blk=blk_at(step)),
            )
        )
        edge_copies.append(
            remote(
                latent_half.at[edge_rows],
                side_view.at[i, edge_place],
                view_send.at[2 + 2 * i],
                view_recv.at[2 + 2 * i],
                at(tube=ahead, blk=blk_at(step)),
            )
        )
    for copy in side_copies:
        copy.start()

    @pl.when(has_ahead)
    def _():
        for copy in edge_copies:
            copy.start()

    view[own_place, :] = latent_half[own_rows, :]
    piece = half // 2
    count_copies = []
    for h in range(2):
        for low in range(0, tubes, 4):
            places = range(low, min(low + 4, tubes))

            def add(c, accs, h=h, places=places, wait=(h == 0 and low == 0)):
                base = pl.multiple_of(c * CHUNK, CHUNK)
                if wait:
                    pltpu.make_async_copy(
                        exposure_ref.at[pl.ds(base, CHUNK)],
                        exposure_buf.at[pl.ds(base, CHUNK)],
                        load_sem.at[c],
                    ).wait()
                picks = [mask[p, pl.ds(base, CHUNK), :] for p in places]
                for q in range(CHUNK):
                    value = exposure_buf[base + q, h * piece : (h + 1) * piece, :].astype(F32)
                    accs = tuple(a + m[q : q + 1, :] * value for a, m in zip(accs, picks))
                return accs

            sums = lax.fori_loop(
                0, slots // CHUNK, add, tuple(jnp.zeros((piece, block), F32) for _ in places)
            )
            for p, value in zip(places, sums):
                count_send[p, h * piece : (h + 1) * piece, :] = value.astype(BF16)
        for j in range(1, tubes):
            p = lax.rem(t + j, tubes)
            part = pl.ds(h * piece, piece)
            count_copies.append(
                remote(
                    count_send.at[p, part],
                    count_recv.at[j - 1, part],
                    count_ssem.at[h, j - 1],
                    count_rsem.at[h, j - 1],
                    at(tube=p),
                )
            )
            count_copies[-1].start()

    tap_copy.wait()
    for i, ref in enumerate((tap_own, tap_other)):
        rounded = ref[...].astype(BF16).astype(F32)
        sums = jnp.sum(rounded, axis=1, keepdims=True)
        scale = 1.0 / (sums[0:kernels] * sums[kernels : 2 * kernels])
        if i == 1:
            weight_copy.wait()
        for k in range(kernels):
            n = i * kernels + k
            along = band(rounded[k : k + 1], HALO - margin, half)
            around = band(rounded[kernels + k : kernels + k + 1], 2 * block - margin, block)
            row_band[n] = along.astype(BF16)
            row_band_t[:, n * half : (n + 1) * half] = along.T[0:ext].astype(BF16)
            col_band[n] = around.astype(BF16)
            if i == 0:
                own = weight_ref[k, pl.ds(pl.multiple_of(s * half, half), half), :]
            else:
                own = weight_other[k]
            scaled[n] = own.astype(F32) * scale[k : k + 1]

    def adjoint(factor):
        for n in range(2 * kernels):
            term = scaled[n] if factor is None else scaled[n] * factor
            spread[n * half : (n + 1) * half, :] = dot(term.astype(BF16), col_band[n]).astype(BF16)
        return dot(row_band_t[...], spread[...])

    lane = lax.broadcasted_iota(jnp.int32, (1, block), 1)
    if blks == 2:
        lanes_of = [(lane < HALO) | (lane >= block - HALO)]
    else:
        lanes_of = [lane < HALO, lane >= block - HALO]

    def exchange(f, value):
        main_send[f] = value[:, 0:block]
        strip_send[f] = value[:, block : 2 * block]
        packed = jnp.zeros((group, block), F32)
        start = pl.multiple_of(o * HALO, HALO)
        for g in range(PACK):
            packed = packed + pltpu.roll(
                strip_send[f, pl.ds(start + g * group, group), :], HALO + 2 * HALO * g, 1
            )
        packed_send[f] = packed
        copies, edges = [], []
        count = 0

        def add(to, src, dst, rsem, device):
            nonlocal count
            to.append(remote(src, dst, field_ssem.at[f, count], rsem, device))
            count += 1

        for i, step in enumerate(sides):
            for sub in (s, o):
                add(
                    copies,
                    packed_send.at[f],
                    packed_recv.at[f, i, s],
                    packed_rsem.at[f, i, s],
                    at(blk=blk_at(step), sub=sub),
                )
                add(
                    edges,
                    strip_send.at[f, edge_place],
                    corner_recv.at[f, i, o],
                    corner_rsem.at[f, i, o],
                    at(tube=behind, blk=blk_at(step), sub=sub),
                )
        for sub in (s, o):
            add(
                edges,
                main_send.at[f, edge_place],
                edge_recv.at[f, o],
                edge_rsem.at[f, o],
                at(tube=behind, sub=sub),
            )
        add(copies, main_send.at[f, own_place], main_recv.at[f], main_rsem.at[f], at(sub=o))
        for copy in copies:
            copy.start()

        @pl.when(has_behind)
        def _():
            for copy in edges:
                copy.start()

        return copies, edges

    def landed(buf, rsem):
        remote(buf, buf, rsem, rsem, at(sub=o)).wait_recv()

    def collect(f):
        other_rows = pl.ds(pl.multiple_of(o * (rows - inner), HALO), inner)
        total[f, edge_rows, :] = jnp.zeros((HALO, block), F32)
        total[f, pl.ds(pl.multiple_of(o * inner, HALO), rows - inner), :] = jnp.zeros(
            (rows - inner, block), F32
        )
        total[f, own_rows, :] = main_send[f, own_place, :]
        landed(main_recv.at[f], main_rsem.at[f])
        total[f, other_rows, :] += main_recv[f]
        for i in range(len(sides)):
            for sub in range(2):
                landed(packed_recv.at[f, i, sub], packed_rsem.at[f, i, sub])
                for g in range(PACK):
                    value = pltpu.roll(
                        packed_recv[f, i, sub], block - (HALO + 2 * HALO * g) % block, 1
                    )
                    start = sub * (rows - inner) + g * group
                    total[f, start : start + group, :] += jnp.where(lanes_of[i], value, 0.0)
        for n, (cond, start) in enumerate(((t > 0, 0), (t < tubes - 1, rows - HALO))):

            @pl.when(cond)
            def _():
                landed(edge_recv.at[f, n], edge_rsem.at[f, n])
                value = edge_recv[f, n]
                for i in range(len(sides)):
                    landed(corner_recv.at[f, i, n], corner_rsem.at[f, i, n])
                    value = value + jnp.where(lanes_of[i], corner_recv[f, i, n], 0.0)
                total[f, start : start + HALO, :] += value

    for copy in side_copies:
        copy.wait_recv()

    @pl.when(has_behind)
    def _():
        for copy in edge_copies:
            copy.wait_recv()

    @pl.when(jnp.logical_not(has_behind))
    def _():
        view[edge_place, :] = jnp.zeros((HALO, block), BF16)
        for i in range(len(sides)):
            side_view[i, edge_place, :] = jnp.zeros((HALO, block), BF16)

    if blks == 2:
        beside = side_view[0]
    else:
        beside = jnp.where(lane < block // 2, side_view[1], side_view[0])
    seen = jnp.concatenate([view[...], beside], axis=1)
    seen = jnp.concatenate([seen, jnp.zeros((2 * block - ext, 2 * block), BF16)], axis=0)
    blurred = jnp.zeros((half, block), F32)
    for n in range(2 * kernels):
        along = dot(row_band[n], seen).astype(BF16)
        both = lax.dot_general(
            along, col_band[n], (((1,), (1,)), ((), ())), preferred_element_type=F32
        )
        blurred = blurred + scaled[n] * both
    inverse = 1.0 / blurred

    coverage = gain_send[t]
    for j, copy in enumerate(gain_copies):
        copy.wait()
        coverage = coverage + gain_recv[j]
    sent_d = exchange(0, adjoint(None) * coverage[0:1, 0:1])
    counts_own = count_send[t].astype(F32)
    collect(0)

    for copy in count_copies:
        copy.wait()
    counts = counts_own
    for j in range(tubes - 1):
        counts = counts + count_recv[j].astype(F32)
    sent_n = exchange(1, adjoint(counts * inverse))
    collect(1)
    out_ref[...] = latent_ref[...] * total[1] / jnp.maximum(total[0], 0.25)

    for copy in side_copies:
        copy.wait_send()

    @pl.when(has_ahead)
    def _():
        for copy in edge_copies:
            copy.wait_send()

    for copies, edges in (sent_d, sent_n):
        for copy in copies:
            copy.wait_send()

        @pl.when(has_behind)
        def _():
            for copy in edges:
                copy.wait_send()


def body(tubes, blks, latent, weight_maps, row_taps, col_taps, exposures, gains, owners, offsets):
    rows, block = latent.shape
    half = rows // 2
    ext = half + 2 * HALO
    inner = half + HALO
    kernels = weight_maps.shape[0]
    slots = exposures.shape[1]
    nside = 1 if blks == 2 else 2
    peers = tubes - 1
    vmem = pl.BlockSpec(memory_space=pltpu.VMEM)
    dma = pltpu.SemaphoreType.DMA
    return pl.pallas_call(
        functools.partial(kernel, tubes, blks),
        out_shape=jax.ShapeDtypeStruct((rows, block), F32),
        in_specs=[vmem] * 4 + [pl.BlockSpec(memory_space=pl.ANY)] + [vmem] * 3,
        out_specs=vmem,
        scratch_shapes=[
            pltpu.VMEM((slots, block, block), BF16),
            pltpu.VMEM((rows, block), BF16),
            pltpu.VMEM((ext, block), BF16),
            pltpu.VMEM((nside, ext, block), BF16),
            pltpu.VMEM((kernels, half, block), BF16),
            pltpu.VMEM((2 * kernels, 2 * block), F32),
            pltpu.VMEM((2 * kernels, 2 * block), F32),
            pltpu.VMEM((tubes, 8, block), F32),
            pltpu.VMEM((peers, 8, block), F32),
            pltpu.VMEM((tubes, slots, block), F32),
            pltpu.VMEM((tubes, half, block), BF16),
            pltpu.VMEM((peers, half, block), BF16),
            pltpu.VMEM((2 * kernels, half, 2 * block), BF16),
            pltpu.VMEM((ext, 2 * kernels * half), BF16),
            pltpu.VMEM((2 * kernels, block, 2 * block), BF16),
            pltpu.VMEM((2 * kernels, half, block), F32),
            pltpu.VMEM((2 * kernels * half, 2 * block), BF16),
            pltpu.VMEM((2, ext, block), F32),
            pltpu.VMEM((2, ext, block), F32),
            pltpu.VMEM((2, inner // PACK, block), F32),
            pltpu.VMEM((2, inner, block), F32),
            pltpu.VMEM((2, 2, HALO, block), F32),
            pltpu.VMEM((2, nside, 2, inner // PACK, block), F32),
            pltpu.VMEM((2, nside, 2, HALO, block), F32),
            pltpu.VMEM((2, rows, block), F32),
            dma((slots // CHUNK,)),
            dma((1 + 2 * nside,)),
            dma((1 + 2 * nside,)),
            dma((2,)),
            dma((2,)),
            dma((peers,)),
            dma((peers,)),
            dma((2, peers)),
            dma((2, peers)),
            dma((2, 4 * nside + 3)),
            dma((2,)),
            dma((2, 2)),
            dma((2, nside, 2)),
            dma((2, nside, 2)),
        ],
        compiler_params=pltpu.CompilerParams(
            collective_id=0, has_side_effects=True, vmem_limit_bytes=40 * 1024 * 1024
        ),
    )(latent, weight_maps, row_taps, col_taps, exposures[0], gains, owners[0], offsets)


def solution(mesh):
    in_specs = (
        P(("sec", "tube"), "blk"),
        P("sub", ("sec", "tube"), "blk"),
        P("sub", None),
        P("sub", None),
        P("blk", ("sec", "tube"), None, None),
        P("blk", ("sec", "tube")),
        P("blk", ("sec", "tube"), None),
        P("blk", ("sec", "tube")),
    )
    out_specs = P(("sec", "tube"), "blk")
    run = functools.partial(body, mesh.shape["tube"], mesh.shape["blk"])
    return jax.shard_map(run, mesh=mesh, in_specs=in_specs, out_specs=out_specs, check_vma=False)
```

```python
import functools

import jax
import jax.numpy as jnp
from jax import lax
from jax.experimental import pallas as pl
from jax.experimental.pallas import tpu as pltpu
from jax.sharding import PartitionSpec as P

MESH = pl.DeviceIdType.MESH
F32 = jnp.float32
BF16 = jnp.bfloat16
HALO = 16
PACK = 3
TILE = 16
PIECES = 2


def dot(a, b):
    return jnp.dot(a, b, preferred_element_type=F32)


def band(base, shift, rows):
    wide = jnp.broadcast_to(base, (rows, base.shape[1]))
    return pltpu.roll(wide, shift, 1, stride=1, stride_axis=0)


def kernel(
    tubes,
    blks,
    latent_hbm,
    weight_hbm,
    row_hbm,
    col_hbm,
    exposure_hbm,
    gain_hbm,
    owner_hbm,
    offset_hbm,
    out_ref,
    exposure_buf,
    latent_ref,
    weight_own,
    row_ref,
    col_ref,
    gain_ref,
    owner_ref,
    offset_ref,
    latent_half,
    view,
    side_view,
    weight_other,
    tap_own,
    tap_other,
    gain_send,
    gain_recv,
    pick,
    count_send,
    count_recv,
    row_band,
    row_band_t,
    col_band,
    scaled,
    spread,
    main_send,
    strip_send,
    packed_send,
    main_recv,
    edge_recv,
    packed_recv,
    corner_recv,
    total,
    load_sem,
    small_sem,
    view_send,
    view_recv,
    weight_sem,
    tap_sem,
    gain_ssem,
    gain_rsem,
    count_ssem,
    count_rsem,
    field_ssem,
    main_rsem,
    edge_rsem,
    packed_rsem,
    corner_rsem,
):
    rows, block = latent_ref.shape
    half = rows // 2
    ext = half + 2 * HALO
    inner = half + HALO
    group = inner // PACK
    kernels = weight_hbm.shape[0]
    taps = row_ref.shape[1]
    margin = taps // 2
    slots = exposure_hbm.shape[0]
    t = lax.axis_index("tube")
    b = lax.axis_index("blk")
    s = lax.axis_index("sub")
    o = 1 - s
    sides = (1,) if blks == 2 else (1, -1)
    ahead = t + 1 - 2 * s
    behind = t - 1 + 2 * s
    has_ahead = (ahead >= 0) & (ahead < tubes)
    has_behind = (behind >= 0) & (behind < tubes)

    def blk_at(step):
        return lax.rem(b + step + blks, blks)

    def at(tube=None, blk=None, sub=None):
        return {
            "tube": t if tube is None else tube,
            "blk": b if blk is None else blk,
            "sub": s if sub is None else sub,
        }

    def remote(src, dst, ssem, rsem, device):
        return pltpu.make_async_remote_copy(
            src_ref=src,
            dst_ref=dst,
            send_sem=ssem,
            recv_sem=rsem,
            device_id=device,
            device_id_type=MESH,
        )

    def load(src, dst, n):
        return pltpu.make_async_copy(src, dst, small_sem.at[n])

    small = [
        load(owner_hbm, owner_ref, 0),
        load(offset_hbm, offset_ref, 1),
        load(gain_hbm, gain_ref, 2),
        load(row_hbm, row_ref, 3),
        load(col_hbm, col_ref, 4),
    ]
    load_latent = load(latent_hbm, latent_ref, 5)
    load_weight = load(
        weight_hbm.at[:, pl.ds(pl.multiple_of(s * half, half), half)], weight_own, 6
    )
    piece = half // PIECES
    loads = [
        pltpu.make_async_copy(
            exposure_hbm.at[:, pl.ds(h * piece, piece)],
            exposure_buf.at[:, pl.ds(h * piece, piece)],
            load_sem.at[h],
        )
        for h in range(PIECES)
    ]
    for copy in small + loads + [load_latent, load_weight]:
        copy.start()

    barrier = pltpu.get_barrier_semaphore()
    near = [0] + list(sides)
    fixed = 0
    for step in near:
        for sub in (s, o):
            if step == 0 and sub is s:
                continue
            pl.semaphore_signal(barrier, inc=1, device_id=at(blk=blk_at(step), sub=sub), device_id_type=MESH)
            fixed += 1
    for j in range(1, tubes):
        pl.semaphore_signal(
            barrier, inc=1, device_id=at(tube=lax.rem(t + j, tubes)), device_id_type=MESH
        )
        fixed += 1
    extra = 2 * len(near) - 1
    for beside in (t - 1, t + 1):

        @pl.when((beside >= 0) & (beside < tubes))
        def _():
            for step in near:
                for sub in (s, o):
                    if step == 0 and sub is s:
                        continue
                    pl.semaphore_signal(
                        barrier,
                        inc=1,
                        device_id=at(tube=beside, blk=blk_at(step), sub=sub),
                        device_id_type=MESH,
                    )

    for copy in small:
        copy.wait()
    tap_own[...] = jnp.zeros_like(tap_own)
    tap_own[0:kernels, 0:taps] = row_ref[...]
    tap_own[kernels : 2 * kernels, 0:taps] = col_ref[...]
    place = (owner_ref[...] * 2 + offset_ref[...]).astype(F32)
    gain = gain_ref[...].astype(F32)
    here = s.astype(F32)
    for p in range(tubes):
        hit = jnp.where(place == here + float(2 * p), gain, 0.0)
        gain_send[p] = jnp.broadcast_to(jnp.sum(hit, axis=1, keepdims=True), (8, block))

    depth = slots * TILE
    slot_of = lax.broadcasted_iota(jnp.int32, (slots, depth), 1) // TILE
    expand = jnp.where(slot_of == lax.broadcasted_iota(jnp.int32, (slots, depth), 0), 1.0, 0.0)
    wide = dot(jnp.broadcast_to(place, (8, slots)).astype(BF16), expand.astype(BF16))[0:1] - here
    same = lax.broadcasted_iota(jnp.int32, (TILE, depth), 1) % TILE == lax.broadcasted_iota(
        jnp.int32, (TILE, depth), 0
    )
    for p in range(tubes):
        pick[p * TILE : (p + 1) * TILE, :] = jnp.where(
            same & (wide == float(2 * p)), 1.0, 0.0
        ).astype(BF16)

    def count_piece(h):
        loads[h].wait()
        for g in range(h * piece // TILE, (h + 1) * piece // TILE):
            part = slice(g * TILE, (g + 1) * TILE)
            sums = dot(pick[...], exposure_buf[:, part, :].reshape(depth, block)).astype(BF16)
            for p in range(tubes):
                count_send[p, part, :] = sums[p * TILE : (p + 1) * TILE]

    count_copies = []

    def send_piece(h):
        for j in range(1, tubes):
            p = lax.rem(t + j, tubes)
            part = pl.ds(h * piece, piece)
            count_copies.append(
                remote(
                    count_send.at[p, part],
                    count_recv.at[j - 1, part],
                    count_ssem.at[h, j - 1],
                    count_rsem.at[h, j - 1],
                    at(tube=p),
                )
            )
            count_copies[-1].start()

    count_piece(0)
    pl.semaphore_wait(
        barrier,
        fixed + extra * ((t > 0).astype(jnp.int32) + (t < tubes - 1).astype(jnp.int32)),
    )
    send_piece(0)

    tap_copy = remote(tap_own, tap_other, tap_sem.at[0], tap_sem.at[1], at(sub=o))
    tap_copy.start()
    weight_copy = remote(
        weight_hbm.at[:, pl.ds(pl.multiple_of(o * half, half), half)],
        weight_other,
        weight_sem.at[0],
        weight_sem.at[1],
        at(sub=o),
    )
    weight_copy.start()
    gain_copies = []
    for j in range(1, tubes):
        p = lax.rem(t + j, tubes)
        gain_copies.append(
            remote(gain_send.at[p], gain_recv.at[j - 1], gain_ssem.at[j - 1], gain_rsem.at[j - 1], at(tube=p))
        )
        gain_copies[-1].start()
    load_latent.wait()
    latent_half[...] = latent_ref[...].astype(BF16)
    own_rows = pl.ds(pl.multiple_of(s * (rows - inner), HALO), inner)
    own_place = pl.ds(pl.multiple_of(o * HALO, HALO), inner)
    edge_rows = pl.ds(pl.multiple_of(o * (rows - HALO), HALO), HALO)
    edge_place = pl.ds(pl.multiple_of(s * inner, HALO), HALO)
    edge_copies = [
        remote(
            latent_half.at[edge_rows],
            view.at[edge_place],
            view_send.at[0],
            view_recv.at[0],
            at(tube=ahead),
        )
    ]
    side_copies = []
    for i, step in enumerate(sides):
        side_copies.append(
            remote(
                latent_half.at[own_rows],
                side_view.at[i, own_place],
                view_send.at[1 + 2 * i],
                view_recv.at[1 + 2 * i],
                at(blk=blk_at(step)),
            )
        )
        edge_copies.append(
            remote(
                latent_half.at[edge_rows],
                side_view.at[i, edge_place],
                view_send.at[2 + 2 * i],
                view_recv.at[2 + 2 * i],
                at(tube=ahead, blk=blk_at(step)),
            )
        )
    for copy in side_copies:
        copy.start()

    @pl.when(has_ahead)
    def _():
        for copy in edge_copies:
            copy.start()

    view[own_place, :] = latent_half[own_rows, :]
    for h in range(1, PIECES):
        count_piece(h)
        send_piece(h)

    load_weight.wait()
    for i, ref in enumerate((tap_own, tap_other)):
        if i == 1:
            tap_copy.wait()
            weight_copy.wait()
        rounded = ref[...].astype(BF16).astype(F32)
        sums = jnp.sum(rounded, axis=1, keepdims=True)
        scale = 1.0 / (sums[0:kernels] * sums[kernels : 2 * kernels])
        for k in range(kernels):
            n = i * kernels + k
            along = band(rounded[k : k + 1], HALO - margin, half)
            around = band(rounded[kernels + k : kernels + k + 1], 2 * block - margin, block)
            row_band[n] = along.astype(BF16)
            row_band_t[:, n * half : (n + 1) * half] = along.T[0:ext].astype(BF16)
            col_band[n] = around.astype(BF16)
            own = weight_own[k] if i == 0 else weight_other[k]
            scaled[n] = own.astype(F32) * scale[k : k + 1]

    def adjoint(factor):
        for n in range(2 * kernels):
            term = scaled[n] if factor is None else scaled[n] * factor
            spread[n * half : (n + 1) * half, :] = dot(term.astype(BF16), col_band[n]).astype(BF16)
        return dot(row_band_t[...], spread[...])

    lane = lax.broadcasted_iota(jnp.int32, (1, block), 1)
    if blks == 2:
        lanes_of = [(lane < HALO) | (lane >= block - HALO)]
    else:
        lanes_of = [lane < HALO, lane >= block - HALO]

    def exchange(f, value):
        main_send[f] = value[:, 0:block]
        strip_send[f] = value[:, block : 2 * block]
        packed = jnp.zeros((group, block), F32)
        start = pl.multiple_of(o * HALO, HALO)
        for g in range(PACK):
            packed = packed + pltpu.roll(
                strip_send[f, pl.ds(start + g * group, group), :], HALO + 2 * HALO * g, 1
            )
        packed_send[f] = packed
        copies, edges = [], []
        count = 0

        def add(to, src, dst, rsem, device):
            nonlocal count
            to.append(remote(src, dst, field_ssem.at[f, count], rsem, device))
            count += 1

        for i, step in enumerate(sides):
            for sub in (s, o):
                add(
                    copies,
                    packed_send.at[f],
                    packed_recv.at[f, i, s],
                    packed_rsem.at[f, i, s],
                    at(blk=blk_at(step), sub=sub),
                )
                add(
                    edges,
                    strip_send.at[f, edge_place],
                    corner_recv.at[f, i, o],
                    corner_rsem.at[f, i, o],
                    at(tube=behind, blk=blk_at(step), sub=sub),
                )
        for sub in (s, o):
            add(
                edges,
                main_send.at[f, edge_place],
                edge_recv.at[f, o],
                edge_rsem.at[f, o],
                at(tube=behind, sub=sub),
            )
        add(copies, main_send.at[f, own_place], main_recv.at[f], main_rsem.at[f], at(sub=o))
        for copy in copies:
            copy.start()

        @pl.when(has_behind)
        def _():
            for copy in edges:
                copy.start()

        return copies, edges

    def landed(buf, rsem):
        remote(buf, buf, rsem, rsem, at(sub=o)).wait_recv()

    def collect(f):
        other_rows = pl.ds(pl.multiple_of(o * (rows - inner), HALO), inner)
        total[f, edge_rows, :] = jnp.zeros((HALO, block), F32)
        total[f, pl.ds(pl.multiple_of(o * inner, HALO), rows - inner), :] = jnp.zeros(
            (rows - inner, block), F32
        )
        total[f, own_rows, :] = main_send[f, own_place, :]
        landed(main_recv.at[f], main_rsem.at[f])
        total[f, other_rows, :] += main_recv[f]
        for i in range(len(sides)):
            for sub in range(2):
                landed(packed_recv.at[f, i, sub], packed_rsem.at[f, i, sub])
                for g in range(PACK):
                    value = pltpu.roll(
                        packed_recv[f, i, sub], block - (HALO + 2 * HALO * g) % block, 1
                    )
                    start = sub * (rows - inner) + g * group
                    total[f, start : start + group, :] += jnp.where(lanes_of[i], value, 0.0)
        for n, (cond, start) in enumerate(((t > 0, 0), (t < tubes - 1, rows - HALO))):

            @pl.when(cond)
            def _():
                landed(edge_recv.at[f, n], edge_rsem.at[f, n])
                value = edge_recv[f, n]
                for i in range(len(sides)):
                    landed(corner_recv.at[f, i, n], corner_rsem.at[f, i, n])
                    value = value + jnp.where(lanes_of[i], corner_recv[f, i, n], 0.0)
                total[f, start : start + HALO, :] += value

    for copy in side_copies:
        copy.wait_recv()

    @pl.when(has_behind)
    def _():
        for copy in edge_copies:
            copy.wait_recv()

    @pl.when(jnp.logical_not(has_behind))
    def _():
        view[edge_place, :] = jnp.zeros((HALO, block), BF16)
        for i in range(len(sides)):
            side_view[i, edge_place, :] = jnp.zeros((HALO, block), BF16)

    if blks == 2:
        beside = side_view[0]
    else:
        beside = jnp.where(lane < block // 2, side_view[1], side_view[0])
    seen = jnp.concatenate([view[...], beside], axis=1)
    seen = jnp.concatenate([seen, jnp.zeros((2 * block - ext, 2 * block), BF16)], axis=0)
    blurred = jnp.zeros((half, block), F32)
    for n in range(2 * kernels):
        along = dot(row_band[n], seen).astype(BF16)
        both = lax.dot_general(
            along, col_band[n], (((1,), (1,)), ((), ())), preferred_element_type=F32
        )
        blurred = blurred + scaled[n] * both
    inverse = 1.0 / blurred

    coverage = gain_send[t]
    for j, copy in enumerate(gain_copies):
        copy.wait()
        coverage = coverage + gain_recv[j]
    sent_d = exchange(0, adjoint(None) * coverage[0:1, 0:1])
    counts_own = count_send[t].astype(F32)
    collect(0)

    for copy in count_copies:
        copy.wait()
    counts = counts_own
    for j in range(tubes - 1):
        counts = counts + count_recv[j].astype(F32)
    sent_n = exchange(1, adjoint(counts * inverse))
    collect(1)
    out_ref[...] = latent_ref[...] * total[1] / jnp.maximum(total[0], 0.25)

    for copy in side_copies:
        copy.wait_send()

    @pl.when(has_ahead)
    def _():
        for copy in edge_copies:
            copy.wait_send()

    for copies, edges in (sent_d, sent_n):
        for copy in copies:
            copy.wait_send()

        @pl.when(has_behind)
        def _():
            for copy in edges:
                copy.wait_send()


def body(tubes, blks, latent, weight_maps, row_taps, col_taps, exposures, gains, owners, offsets):
    rows, block = latent.shape
    half = rows // 2
    ext = half + 2 * HALO
    inner = half + HALO
    kernels = weight_maps.shape[0]
    slots = exposures.shape[1]
    nside = 1 if blks == 2 else 2
    peers = tubes - 1
    vmem = pl.BlockSpec(memory_space=pltpu.VMEM)
    anywhere = pl.BlockSpec(memory_space=pl.ANY)
    taps = row_taps.shape[1]
    dma = pltpu.SemaphoreType.DMA
    return pl.pallas_call(
        functools.partial(kernel, tubes, blks),
        out_shape=jax.ShapeDtypeStruct((rows, block), F32),
        in_specs=[anywhere] * 8,
        out_specs=vmem,
        scratch_shapes=[
            pltpu.VMEM((slots, block, block), BF16),
            pltpu.VMEM((rows, block), F32),
            pltpu.VMEM((kernels, half, block), BF16),
            pltpu.VMEM((kernels, taps), F32),
            pltpu.VMEM((kernels, taps), F32),
            pltpu.VMEM((1, slots), BF16),
            pltpu.VMEM((1, slots), jnp.int32),
            pltpu.VMEM((1, slots), jnp.int32),
            pltpu.VMEM((rows, block), BF16),
            pltpu.VMEM((ext, block), BF16),
            pltpu.VMEM((nside, ext, block), BF16),
            pltpu.VMEM((kernels, half, block), BF16),
            pltpu.VMEM((2 * kernels, 2 * block), F32),
            pltpu.VMEM((2 * kernels, 2 * block), F32),
            pltpu.VMEM((tubes, 8, block), F32),
            pltpu.VMEM((peers, 8, block), F32),
            pltpu.VMEM((tubes * TILE, slots * TILE), BF16),
            pltpu.VMEM((tubes, half, block), BF16),
            pltpu.VMEM((peers, half, block), BF16),
            pltpu.VMEM((2 * kernels, half, 2 * block), BF16),
            pltpu.VMEM((ext, 2 * kernels * half), BF16),
            pltpu.VMEM((2 * kernels, block, 2 * block), BF16),
            pltpu.VMEM((2 * kernels, half, block), F32),
            pltpu.VMEM((2 * kernels * half, 2 * block), BF16),
            pltpu.VMEM((2, ext, block), F32),
            pltpu.VMEM((2, ext, block), F32),
            pltpu.VMEM((2, inner // PACK, block), F32),
            pltpu.VMEM((2, inner, block), F32),
            pltpu.VMEM((2, 2, HALO, block), F32),
            pltpu.VMEM((2, nside, 2, inner // PACK, block), F32),
            pltpu.VMEM((2, nside, 2, HALO, block), F32),
            pltpu.VMEM((2, rows, block), F32),
            dma((PIECES,)),
            dma((7,)),
            dma((1 + 2 * nside,)),
            dma((1 + 2 * nside,)),
            dma((2,)),
            dma((2,)),
            dma((peers,)),
            dma((peers,)),
            dma((PIECES, peers)),
            dma((PIECES, peers)),
            dma((2, 4 * nside + 3)),
            dma((2,)),
            dma((2, 2)),
            dma((2, nside, 2)),
            dma((2, nside, 2)),
        ],
        compiler_params=pltpu.CompilerParams(
            collective_id=0, has_side_effects=True, vmem_limit_bytes=60 * 1024 * 1024
        ),
    )(latent, weight_maps, row_taps, col_taps, exposures[0], gains, owners.reshape(1, slots), offsets)


def solution(mesh):
    in_specs = (
        P(("sec", "tube"), "blk"),
        P("sub", ("sec", "tube"), "blk"),
        P("sub", None),
        P("sub", None),
        P("blk", ("sec", "tube"), None, None),
        P("blk", ("sec", "tube")),
        P("blk", ("sec", "tube"), None),
        P("blk", ("sec", "tube")),
    )
    out_specs = P(("sec", "tube"), "blk")
    run = functools.partial(body, mesh.shape["tube"], mesh.shape["blk"])
    return jax.shard_map(run, mesh=mesh, in_specs=in_specs, out_specs=out_specs, check_vma=False)
```

```python
import functools

import jax
import jax.numpy as jnp
from jax import lax
from jax.experimental import pallas as pl
from jax.experimental.pallas import tpu as pltpu
from jax.sharding import PartitionSpec as P

MESH = pl.DeviceIdType.MESH
F32 = jnp.float32
BF16 = jnp.bfloat16
HALO = 16
PACK = 3
TILE = 16
PIECES = 2


def dot(a, b):
    return jnp.dot(a, b, preferred_element_type=F32)


def band(base, shift, rows):
    wide = jnp.broadcast_to(base, (rows, base.shape[1]))
    return pltpu.roll(wide, shift, 1, stride=1, stride_axis=0)


def kernel(
    tubes,
    blks,
    latent_hbm,
    weight_hbm,
    row_hbm,
    col_hbm,
    exposure_hbm,
    gain_hbm,
    owner_hbm,
    offset_hbm,
    out_ref,
    exposure_buf,
    latent_ref,
    weight_own,
    row_ref,
    col_ref,
    gain_ref,
    owner_ref,
    offset_ref,
    latent_half,
    view,
    side_view,
    weight_other,
    tap_own,
    tap_other,
    gain_send,
    gain_recv,
    pick,
    count_send,
    count_recv,
    row_band,
    row_band_t,
    col_band,
    scaled,
    spread,
    main_send,
    strip_send,
    packed_send,
    main_recv,
    edge_recv,
    packed_recv,
    corner_recv,
    total,
    load_sem,
    small_sem,
    view_send,
    view_recv,
    weight_sem,
    tap_sem,
    gain_ssem,
    gain_rsem,
    count_ssem,
    count_rsem,
    field_ssem,
    main_rsem,
    edge_rsem,
    packed_rsem,
    corner_rsem,
):
    rows, block = latent_ref.shape
    half = rows // 2
    ext = half + 2 * HALO
    inner = half + HALO
    group = inner // PACK
    kernels = weight_hbm.shape[0]
    taps = row_ref.shape[1]
    margin = taps // 2
    slots = exposure_hbm.shape[0]
    t = lax.axis_index("tube")
    b = lax.axis_index("blk")
    s = lax.axis_index("sub")
    o = 1 - s
    sides = (1,) if blks == 2 else (1, -1)
    ahead = t + 1 - 2 * s
    behind = t - 1 + 2 * s
    has_ahead = (ahead >= 0) & (ahead < tubes)
    has_behind = (behind >= 0) & (behind < tubes)

    def blk_at(step):
        return lax.rem(b + step + blks, blks)

    def at(tube=None, blk=None, sub=None):
        return {
            "tube": t if tube is None else tube,
            "blk": b if blk is None else blk,
            "sub": s if sub is None else sub,
        }

    def remote(src, dst, ssem, rsem, device):
        return pltpu.make_async_remote_copy(
            src_ref=src,
            dst_ref=dst,
            send_sem=ssem,
            recv_sem=rsem,
            device_id=device,
            device_id_type=MESH,
        )

    def load(src, dst, n):
        return pltpu.make_async_copy(src, dst, small_sem.at[n])

    small = [
        load(owner_hbm, owner_ref, 0),
        load(offset_hbm, offset_ref, 1),
        load(gain_hbm, gain_ref, 2),
        load(row_hbm, row_ref, 3),
        load(col_hbm, col_ref, 4),
    ]
    load_latent = load(latent_hbm, latent_ref, 5)
    load_weight = load(
        weight_hbm.at[:, pl.ds(pl.multiple_of(s * half, half), half)], weight_own, 6
    )
    piece = half // PIECES
    loads = [
        pltpu.make_async_copy(
            exposure_hbm.at[:, pl.ds(h * piece, piece)],
            exposure_buf.at[:, pl.ds(h * piece, piece)],
            load_sem.at[h],
        )
        for h in range(PIECES)
    ]
    for copy in small + loads + [load_latent, load_weight]:
        copy.start()

    barrier = pltpu.get_barrier_semaphore()
    near = [0] + list(sides)
    fixed = 0
    for step in near:
        for sub in (s, o):
            if step == 0 and sub is s:
                continue
            pl.semaphore_signal(barrier, inc=1, device_id=at(blk=blk_at(step), sub=sub), device_id_type=MESH)
            fixed += 1
    for j in range(1, tubes):
        pl.semaphore_signal(
            barrier, inc=1, device_id=at(tube=lax.rem(t + j, tubes)), device_id_type=MESH
        )
        fixed += 1
    extra = 2 * len(near) - 1
    for beside in (t - 1, t + 1):

        @pl.when((beside >= 0) & (beside < tubes))
        def _():
            for step in near:
                for sub in (s, o):
                    if step == 0 and sub is s:
                        continue
                    pl.semaphore_signal(
                        barrier,
                        inc=1,
                        device_id=at(tube=beside, blk=blk_at(step), sub=sub),
                        device_id_type=MESH,
                    )

    for copy in small:
        copy.wait()
    tap_own[...] = jnp.zeros_like(tap_own)
    tap_own[0:kernels, 0:taps] = row_ref[...]
    tap_own[kernels : 2 * kernels, 0:taps] = col_ref[...]
    place = (owner_ref[...] * 2 + offset_ref[...]).astype(F32)
    gain = gain_ref[...].astype(F32)
    here = s.astype(F32)
    for p in range(tubes):
        hit = jnp.where(place == here + float(2 * p), gain, 0.0)
        gain_send[p] = jnp.broadcast_to(jnp.sum(hit, axis=1, keepdims=True), (8, block))

    depth = slots * TILE
    slot_of = lax.broadcasted_iota(jnp.int32, (slots, depth), 1) // TILE
    expand = jnp.where(slot_of == lax.broadcasted_iota(jnp.int32, (slots, depth), 0), 1.0, 0.0)
    wide = dot(jnp.broadcast_to(place, (8, slots)).astype(BF16), expand.astype(BF16))[0:1] - here
    same = lax.broadcasted_iota(jnp.int32, (TILE, depth), 1) % TILE == lax.broadcasted_iota(
        jnp.int32, (TILE, depth), 0
    )
    for p in range(tubes):
        pick[p * TILE : (p + 1) * TILE, :] = jnp.where(
            same & (wide == float(2 * p)), 1.0, 0.0
        ).astype(BF16)

    def count_piece(h):
        loads[h].wait()
        for g in range(h * piece // TILE, (h + 1) * piece // TILE):
            part = slice(g * TILE, (g + 1) * TILE)
            sums = dot(pick[...], exposure_buf[:, part, :].reshape(depth, block)).astype(BF16)
            for p in range(tubes):
                count_send[p, part, :] = sums[p * TILE : (p + 1) * TILE]

    count_copies = []

    def send_piece(h):
        for j in range(1, tubes):
            p = lax.rem(t + j, tubes)
            part = pl.ds(h * piece, piece)
            count_copies.append(
                remote(
                    count_send.at[p, part],
                    count_recv.at[j - 1, part],
                    count_ssem.at[h, j - 1],
                    count_rsem.at[h, j - 1],
                    at(tube=p),
                )
            )
            count_copies[-1].start()

    count_piece(0)
    pl.semaphore_wait(
        barrier,
        fixed + extra * ((t > 0).astype(jnp.int32) + (t < tubes - 1).astype(jnp.int32)),
    )
    send_piece(0)

    tap_copy = remote(tap_own, tap_other, tap_sem.at[0], tap_sem.at[1], at(sub=o))
    tap_copy.start()
    weight_copy = remote(
        weight_hbm.at[:, pl.ds(pl.multiple_of(o * half, half), half)],
        weight_other,
        weight_sem.at[0],
        weight_sem.at[1],
        at(sub=o),
    )
    weight_copy.start()
    gain_copies = []
    for j in range(1, tubes):
        p = lax.rem(t + j, tubes)
        gain_copies.append(
            remote(gain_send.at[p], gain_recv.at[j - 1], gain_ssem.at[j - 1], gain_rsem.at[j - 1], at(tube=p))
        )
        gain_copies[-1].start()
    load_latent.wait()
    latent_half[...] = latent_ref[...].astype(BF16)
    own_rows = pl.ds(pl.multiple_of(s * (rows - inner), HALO), inner)
    own_place = pl.ds(pl.multiple_of(o * HALO, HALO), inner)
    edge_rows = pl.ds(pl.multiple_of(o * (rows - HALO), HALO), HALO)
    edge_place = pl.ds(pl.multiple_of(s * inner, HALO), HALO)
    edge_copies = [
        remote(
            latent_half.at[edge_rows],
            view.at[edge_place],
            view_send.at[0],
            view_recv.at[0],
            at(tube=ahead),
        )
    ]
    side_copies = []
    for i, step in enumerate(sides):
        side_copies.append(
            remote(
                latent_half.at[own_rows],
                side_view.at[i, own_place],
                view_send.at[1 + 2 * i],
                view_recv.at[1 + 2 * i],
                at(blk=blk_at(step)),
            )
        )
        edge_copies.append(
            remote(
                latent_half.at[edge_rows],
                side_view.at[i, edge_place],
                view_send.at[2 + 2 * i],
                view_recv.at[2 + 2 * i],
                at(tube=ahead, blk=blk_at(step)),
            )
        )
    for copy in side_copies:
        copy.start()

    @pl.when(has_ahead)
    def _():
        for copy in edge_copies:
            copy.start()

    view[own_place, :] = latent_half[own_rows, :]
    for h in range(1, PIECES):
        count_piece(h)
        send_piece(h)

    load_weight.wait()
    for i, ref in enumerate((tap_own, tap_other)):
        if i == 1:
            tap_copy.wait()
            weight_copy.wait()
        rounded = ref[...].astype(BF16).astype(F32)
        sums = jnp.sum(rounded, axis=1, keepdims=True)
        scale = 1.0 / (sums[0:kernels] * sums[kernels : 2 * kernels])
        for k in range(kernels):
            n = i * kernels + k
            along = band(rounded[k : k + 1], HALO - margin, half)
            around = band(rounded[kernels + k : kernels + k + 1], 2 * block - margin, block)
            row_band[n] = along.astype(BF16)
            row_band_t[:, n * half : (n + 1) * half] = along.T[0:ext].astype(BF16)
            col_band[n] = around.astype(BF16)
            own = weight_own[k] if i == 0 else weight_other[k]
            scaled[n] = own.astype(F32) * scale[k : k + 1]

    def adjoint(factor):
        for n in range(2 * kernels):
            term = scaled[n] if factor is None else scaled[n] * factor
            spread[n * half : (n + 1) * half, :] = dot(term.astype(BF16), col_band[n]).astype(BF16)
        return dot(row_band_t[...], spread[...])

    lane = lax.broadcasted_iota(jnp.int32, (1, block), 1)
    if blks == 2:
        lanes_of = [(lane < HALO) | (lane >= block - HALO)]
    else:
        lanes_of = [lane < HALO, lane >= block - HALO]

    def exchange(f, value):
        main_send[f] = value[:, 0:block]
        strip_send[f] = value[:, block : 2 * block]
        packed = jnp.zeros((group, block), F32)
        start = pl.multiple_of(o * HALO, HALO)
        for g in range(PACK):
            packed = packed + pltpu.roll(
                strip_send[f, pl.ds(start + g * group, group), :], HALO + 2 * HALO * g, 1
            )
        packed_send[f] = packed
        copies, edges = [], []
        count = 0

        def add(to, src, dst, rsem, device):
            nonlocal count
            to.append(remote(src, dst, field_ssem.at[f, count], rsem, device))
            count += 1

        for i, step in enumerate(sides):
            for sub in (s, o):
                add(
                    copies,
                    packed_send.at[f],
                    packed_recv.at[f, i, s],
                    packed_rsem.at[f, i, s],
                    at(blk=blk_at(step), sub=sub),
                )
                add(
                    edges,
                    strip_send.at[f, edge_place],
                    corner_recv.at[f, i, o],
                    corner_rsem.at[f, i, o],
                    at(tube=behind, blk=blk_at(step), sub=sub),
                )
        for sub in (s, o):
            add(
                edges,
                main_send.at[f, edge_place],
                edge_recv.at[f, o],
                edge_rsem.at[f, o],
                at(tube=behind, sub=sub),
            )
        add(copies, main_send.at[f, own_place], main_recv.at[f], main_rsem.at[f], at(sub=o))
        for copy in copies:
            copy.start()

        @pl.when(has_behind)
        def _():
            for copy in edges:
                copy.start()

        return copies, edges

    def landed(buf, rsem):
        remote(buf, buf, rsem, rsem, at(sub=o)).wait_recv()

    def collect(f):
        other_rows = pl.ds(pl.multiple_of(o * (rows - inner), HALO), inner)
        total[f, edge_rows, :] = jnp.zeros((HALO, block), F32)
        total[f, pl.ds(pl.multiple_of(o * inner, HALO), rows - inner), :] = jnp.zeros(
            (rows - inner, block), F32
        )
        total[f, own_rows, :] = main_send[f, own_place, :]
        landed(main_recv.at[f], main_rsem.at[f])
        total[f, other_rows, :] += main_recv[f]
        for i in range(len(sides)):
            for sub in range(2):
                landed(packed_recv.at[f, i, sub], packed_rsem.at[f, i, sub])
                for g in range(PACK):
                    value = pltpu.roll(
                        packed_recv[f, i, sub], block - (HALO + 2 * HALO * g) % block, 1
                    )
                    start = sub * (rows - inner) + g * group
                    total[f, start : start + group, :] += jnp.where(lanes_of[i], value, 0.0)
        for n, (cond, start) in enumerate(((t > 0, 0), (t < tubes - 1, rows - HALO))):

            @pl.when(cond)
            def _():
                landed(edge_recv.at[f, n], edge_rsem.at[f, n])
                value = edge_recv[f, n]
                for i in range(len(sides)):
                    landed(corner_recv.at[f, i, n], corner_rsem.at[f, i, n])
                    value = value + jnp.where(lanes_of[i], corner_recv[f, i, n], 0.0)
                total[f, start : start + HALO, :] += value

    coverage = gain_send[t]
    for j, copy in enumerate(gain_copies):
        copy.wait()
        coverage = coverage + gain_recv[j]
    sent_d = exchange(0, adjoint(None) * coverage[0:1, 0:1])

    for copy in side_copies:
        copy.wait_recv()

    @pl.when(has_behind)
    def _():
        for copy in edge_copies:
            copy.wait_recv()

    @pl.when(jnp.logical_not(has_behind))
    def _():
        view[edge_place, :] = jnp.zeros((HALO, block), BF16)
        for i in range(len(sides)):
            side_view[i, edge_place, :] = jnp.zeros((HALO, block), BF16)

    if blks == 2:
        beside = side_view[0]
    else:
        beside = jnp.where(lane < block // 2, side_view[1], side_view[0])
    seen = jnp.concatenate([view[...], beside], axis=1)
    seen = jnp.concatenate([seen, jnp.zeros((2 * block - ext, 2 * block), BF16)], axis=0)
    blurred = jnp.zeros((half, block), F32)
    for n in range(2 * kernels):
        along = dot(row_band[n], seen).astype(BF16)
        both = lax.dot_general(
            along, col_band[n], (((1,), (1,)), ((), ())), preferred_element_type=F32
        )
        blurred = blurred + scaled[n] * both
    inverse = 1.0 / blurred

    for copy in count_copies:
        copy.wait()
    counts = count_send[t].astype(F32)
    for j in range(tubes - 1):
        counts = counts + count_recv[j].astype(F32)
    sent_n = exchange(1, adjoint(counts * inverse))
    collect(0)
    collect(1)
    out_ref[...] = latent_ref[...] * total[1] / jnp.maximum(total[0], 0.25)

    for copy in side_copies:
        copy.wait_send()

    @pl.when(has_ahead)
    def _():
        for copy in edge_copies:
            copy.wait_send()

    for copies, edges in (sent_d, sent_n):
        for copy in copies:
            copy.wait_send()

        @pl.when(has_behind)
        def _():
            for copy in edges:
                copy.wait_send()


def body(tubes, blks, latent, weight_maps, row_taps, col_taps, exposures, gains, owners, offsets):
    rows, block = latent.shape
    half = rows // 2
    ext = half + 2 * HALO
    inner = half + HALO
    kernels = weight_maps.shape[0]
    slots = exposures.shape[1]
    nside = 1 if blks == 2 else 2
    peers = tubes - 1
    vmem = pl.BlockSpec(memory_space=pltpu.VMEM)
    anywhere = pl.BlockSpec(memory_space=pl.ANY)
    taps = row_taps.shape[1]
    dma = pltpu.SemaphoreType.DMA
    return pl.pallas_call(
        functools.partial(kernel, tubes, blks),
        out_shape=jax.ShapeDtypeStruct((rows, block), F32),
        in_specs=[anywhere] * 8,
        out_specs=vmem,
        scratch_shapes=[
            pltpu.VMEM((slots, block, block), BF16),
            pltpu.VMEM((rows, block), F32),
            pltpu.VMEM((kernels, half, block), BF16),
            pltpu.VMEM((kernels, taps), F32),
            pltpu.VMEM((kernels, taps), F32),
            pltpu.VMEM((1, slots), BF16),
            pltpu.VMEM((1, slots), jnp.int32),
            pltpu.VMEM((1, slots), jnp.int32),
            pltpu.VMEM((rows, block), BF16),
            pltpu.VMEM((ext, block), BF16),
            pltpu.VMEM((nside, ext, block), BF16),
            pltpu.VMEM((kernels, half, block), BF16),
            pltpu.VMEM((2 * kernels, 2 * block), F32),
            pltpu.VMEM((2 * kernels, 2 * block), F32),
            pltpu.VMEM((tubes, 8, block), F32),
            pltpu.VMEM((peers, 8, block), F32),
            pltpu.VMEM((tubes * TILE, slots * TILE), BF16),
            pltpu.VMEM((tubes, half, block), BF16),
            pltpu.VMEM((peers, half, block), BF16),
            pltpu.VMEM((2 * kernels, half, 2 * block), BF16),
            pltpu.VMEM((ext, 2 * kernels * half), BF16),
            pltpu.VMEM((2 * kernels, block, 2 * block), BF16),
            pltpu.VMEM((2 * kernels, half, block), F32),
            pltpu.VMEM((2 * kernels * half, 2 * block), BF16),
            pltpu.VMEM((2, ext, block), F32),
            pltpu.VMEM((2, ext, block), F32),
            pltpu.VMEM((2, inner // PACK, block), F32),
            pltpu.VMEM((2, inner, block), F32),
            pltpu.VMEM((2, 2, HALO, block), F32),
            pltpu.VMEM((2, nside, 2, inner // PACK, block), F32),
            pltpu.VMEM((2, nside, 2, HALO, block), F32),
            pltpu.VMEM((2, rows, block), F32),
            dma((PIECES,)),
            dma((7,)),
            dma((1 + 2 * nside,)),
            dma((1 + 2 * nside,)),
            dma((2,)),
            dma((2,)),
            dma((peers,)),
            dma((peers,)),
            dma((PIECES, peers)),
            dma((PIECES, peers)),
            dma((2, 4 * nside + 3)),
            dma((2,)),
            dma((2, 2)),
            dma((2, nside, 2)),
            dma((2, nside, 2)),
        ],
        compiler_params=pltpu.CompilerParams(
            collective_id=0, has_side_effects=True, vmem_limit_bytes=60 * 1024 * 1024
        ),
    )(latent, weight_maps, row_taps, col_taps, exposures[0], gains, owners.reshape(1, slots), offsets)


def solution(mesh):
    in_specs = (
        P(("sec", "tube"), "blk"),
        P("sub", ("sec", "tube"), "blk"),
        P("sub", None),
        P("sub", None),
        P("blk", ("sec", "tube"), None, None),
        P("blk", ("sec", "tube")),
        P("blk", ("sec", "tube"), None),
        P("blk", ("sec", "tube")),
    )
    out_specs = P(("sec", "tube"), "blk")
    run = functools.partial(body, mesh.shape["tube"], mesh.shape["blk"])
    return jax.shard_map(run, mesh=mesh, in_specs=in_specs, out_specs=out_specs, check_vma=False)
```

```python
import functools

import jax
import jax.numpy as jnp
from jax import lax
from jax.experimental import pallas as pl
from jax.experimental.pallas import tpu as pltpu
from jax.sharding import PartitionSpec as P

MESH = pl.DeviceIdType.MESH
F32 = jnp.float32
BF16 = jnp.bfloat16
HALO = 16
PACK = 3
TILE = 16
PIECES = 4


def dot(a, b):
    return jnp.dot(a, b, preferred_element_type=F32)


def band(base, shift, rows):
    wide = jnp.broadcast_to(base, (rows, base.shape[1]))
    return pltpu.roll(wide, shift, 1, stride=1, stride_axis=0)


def kernel(
    tubes,
    blks,
    latent_hbm,
    weight_hbm,
    row_hbm,
    col_hbm,
    exposure_hbm,
    gain_hbm,
    owner_hbm,
    offset_hbm,
    out_ref,
    exposure_buf,
    latent_ref,
    weight_own,
    row_ref,
    col_ref,
    gain_ref,
    owner_ref,
    offset_ref,
    latent_half,
    view,
    side_view,
    weight_other,
    tap_own,
    tap_other,
    gain_send,
    gain_recv,
    pick,
    count_send,
    count_recv,
    row_band,
    row_band_t,
    col_band,
    scaled,
    spread,
    main_send,
    strip_send,
    packed_send,
    main_recv,
    edge_recv,
    packed_recv,
    corner_recv,
    total,
    load_sem,
    small_sem,
    view_send,
    view_recv,
    weight_sem,
    tap_sem,
    gain_ssem,
    gain_rsem,
    count_ssem,
    count_rsem,
    field_ssem,
    main_rsem,
    edge_rsem,
    packed_rsem,
    corner_rsem,
):
    rows, block = latent_ref.shape
    half = rows // 2
    ext = half + 2 * HALO
    inner = half + HALO
    group = inner // PACK
    kernels = weight_hbm.shape[0]
    taps = row_ref.shape[1]
    margin = taps // 2
    slots = exposure_hbm.shape[0]
    t = lax.axis_index("tube")
    b = lax.axis_index("blk")
    s = lax.axis_index("sub")
    o = 1 - s
    sides = (1,) if blks == 2 else (1, -1)
    ahead = t + 1 - 2 * s
    behind = t - 1 + 2 * s
    has_ahead = (ahead >= 0) & (ahead < tubes)
    has_behind = (behind >= 0) & (behind < tubes)

    def blk_at(step):
        return lax.rem(b + step + blks, blks)

    def at(tube=None, blk=None, sub=None):
        return {
            "tube": t if tube is None else tube,
            "blk": b if blk is None else blk,
            "sub": s if sub is None else sub,
        }

    def remote(src, dst, ssem, rsem, device):
        return pltpu.make_async_remote_copy(
            src_ref=src,
            dst_ref=dst,
            send_sem=ssem,
            recv_sem=rsem,
            device_id=device,
            device_id_type=MESH,
        )

    barrier = pltpu.get_barrier_semaphore()
    near = [0] + list(sides)
    fixed = 0
    for step in near:
        for sub in (s, o):
            if step == 0 and sub is s:
                continue
            pl.semaphore_signal(barrier, inc=1, device_id=at(blk=blk_at(step), sub=sub), device_id_type=MESH)
            fixed += 1
    for j in range(1, tubes):
        pl.semaphore_signal(
            barrier, inc=1, device_id=at(tube=lax.rem(t + j, tubes)), device_id_type=MESH
        )
        fixed += 1
    extra = 2 * len(near) - 1
    for beside in (t - 1, t + 1):

        @pl.when((beside >= 0) & (beside < tubes))
        def _():
            for step in near:
                for sub in (s, o):
                    if step == 0 and sub is s:
                        continue
                    pl.semaphore_signal(
                        barrier,
                        inc=1,
                        device_id=at(tube=beside, blk=blk_at(step), sub=sub),
                        device_id_type=MESH,
                    )

    def load(src, dst, n):
        return pltpu.make_async_copy(src, dst, small_sem.at[n])

    small = [
        load(owner_hbm, owner_ref, 0),
        load(offset_hbm, offset_ref, 1),
        load(gain_hbm, gain_ref, 2),
        load(row_hbm, row_ref, 3),
        load(col_hbm, col_ref, 4),
    ]
    load_latent = load(latent_hbm, latent_ref, 5)
    load_weight = load(
        weight_hbm.at[:, pl.ds(pl.multiple_of(s * half, half), half)], weight_own, 6
    )
    piece = half // PIECES
    loads = [
        pltpu.make_async_copy(
            exposure_hbm.at[:, pl.ds(h * piece, piece)],
            exposure_buf.at[:, pl.ds(h * piece, piece)],
            load_sem.at[h],
        )
        for h in range(PIECES)
    ]
    for copy in small + loads + [load_latent, load_weight]:
        copy.start()

    for copy in small:
        copy.wait()
    tap_own[...] = jnp.zeros_like(tap_own)
    tap_own[0:kernels, 0:taps] = row_ref[...]
    tap_own[kernels : 2 * kernels, 0:taps] = col_ref[...]
    place = (owner_ref[...] * 2 + offset_ref[...]).astype(F32)
    gain = gain_ref[...].astype(F32)
    here = s.astype(F32)
    for p in range(tubes):
        hit = jnp.where(place == here + float(2 * p), gain, 0.0)
        gain_send[p] = jnp.broadcast_to(jnp.sum(hit, axis=1, keepdims=True), (8, block))

    depth = slots * TILE
    slot_of = lax.broadcasted_iota(jnp.int32, (slots, depth), 1) // TILE
    expand = jnp.where(slot_of == lax.broadcasted_iota(jnp.int32, (slots, depth), 0), 1.0, 0.0)
    wide = dot(jnp.broadcast_to(place, (8, slots)).astype(BF16), expand.astype(BF16))[0:1] - here
    same = lax.broadcasted_iota(jnp.int32, (TILE, depth), 1) % TILE == lax.broadcasted_iota(
        jnp.int32, (TILE, depth), 0
    )
    for p in range(tubes):
        pick[p * TILE : (p + 1) * TILE, :] = jnp.where(
            same & (wide == float(2 * p)), 1.0, 0.0
        ).astype(BF16)

    def count_piece(h):
        loads[h].wait()
        for g in range(h * piece // TILE, (h + 1) * piece // TILE):
            part = slice(g * TILE, (g + 1) * TILE)
            sums = dot(pick[...], exposure_buf[:, part, :].reshape(depth, block)).astype(BF16)
            for p in range(tubes):
                count_send[p, part, :] = sums[p * TILE : (p + 1) * TILE]

    count_copies, gain_copies = [], []

    def send_piece(h):
        for j in range(1, tubes):
            p = lax.rem(t + j, tubes)
            part = pl.ds(h * piece, piece)
            count_copies.append(
                remote(
                    count_send.at[p, part],
                    count_recv.at[j - 1, part],
                    count_ssem.at[h, j - 1],
                    count_rsem.at[h, j - 1],
                    at(tube=p),
                )
            )
            count_copies[-1].start()

    count_piece(0)
    pl.semaphore_wait(
        barrier,
        fixed + extra * ((t > 0).astype(jnp.int32) + (t < tubes - 1).astype(jnp.int32)),
    )
    for j in range(1, tubes):
        p = lax.rem(t + j, tubes)
        gain_copies.append(
            remote(gain_send.at[p], gain_recv.at[j - 1], gain_ssem.at[j - 1], gain_rsem.at[j - 1], at(tube=p))
        )
        gain_copies[-1].start()
    send_piece(0)

    tap_copy = remote(tap_own, tap_other, tap_sem.at[0], tap_sem.at[1], at(sub=o))
    tap_copy.start()
    weight_copy = remote(
        weight_hbm.at[:, pl.ds(pl.multiple_of(o * half, half), half)],
        weight_other,
        weight_sem.at[0],
        weight_sem.at[1],
        at(sub=o),
    )
    weight_copy.start()
    load_latent.wait()
    latent_half[...] = latent_ref[...].astype(BF16)
    own_rows = pl.ds(pl.multiple_of(s * (rows - inner), HALO), inner)
    own_place = pl.ds(pl.multiple_of(o * HALO, HALO), inner)
    edge_rows = pl.ds(pl.multiple_of(o * (rows - HALO), HALO), HALO)
    edge_place = pl.ds(pl.multiple_of(s * inner, HALO), HALO)
    edge_copies = [
        remote(
            latent_half.at[edge_rows],
            view.at[edge_place],
            view_send.at[0],
            view_recv.at[0],
            at(tube=ahead),
        )
    ]
    side_copies = []
    for i, step in enumerate(sides):
        side_copies.append(
            remote(
                latent_half.at[own_rows],
                side_view.at[i, own_place],
                view_send.at[1 + 2 * i],
                view_recv.at[1 + 2 * i],
                at(blk=blk_at(step)),
            )
        )
        edge_copies.append(
            remote(
                latent_half.at[edge_rows],
                side_view.at[i, edge_place],
                view_send.at[2 + 2 * i],
                view_recv.at[2 + 2 * i],
                at(tube=ahead, blk=blk_at(step)),
            )
        )
    for copy in side_copies:
        copy.start()

    @pl.when(has_ahead)
    def _():
        for copy in edge_copies:
            copy.start()

    view[own_place, :] = latent_half[own_rows, :]
    for h in range(1, PIECES):
        count_piece(h)
        send_piece(h)

    load_weight.wait()
    for i, ref in enumerate((tap_own, tap_other)):
        if i == 1:
            tap_copy.wait()
            weight_copy.wait()
        rounded = ref[...].astype(BF16).astype(F32)
        sums = jnp.sum(rounded, axis=1, keepdims=True)
        scale = 1.0 / (sums[0:kernels] * sums[kernels : 2 * kernels])
        for k in range(kernels):
            n = i * kernels + k
            along = band(rounded[k : k + 1], HALO - margin, half)
            around = band(rounded[kernels + k : kernels + k + 1], 2 * block - margin, block)
            row_band[n] = along.astype(BF16)
            row_band_t[:, n * half : (n + 1) * half] = along.T[0:ext].astype(BF16)
            col_band[n] = around.astype(BF16)
            own = weight_own[k] if i == 0 else weight_other[k]
            scaled[n] = own.astype(F32) * scale[k : k + 1]

    def adjoint(factor):
        for n in range(2 * kernels):
            term = scaled[n] if factor is None else scaled[n] * factor
            spread[n * half : (n + 1) * half, :] = dot(term.astype(BF16), col_band[n]).astype(BF16)
        return dot(row_band_t[...], spread[...])

    lane = lax.broadcasted_iota(jnp.int32, (1, block), 1)
    if blks == 2:
        lanes_of = [(lane < HALO) | (lane >= block - HALO)]
    else:
        lanes_of = [lane < HALO, lane >= block - HALO]

    def exchange(f, value):
        main_send[f] = value[:, 0:block]
        strip_send[f] = value[:, block : 2 * block]
        copies, edges = [], []
        count = 0

        def add(to, src, dst, rsem, device):
            nonlocal count
            to.append(remote(src, dst, field_ssem.at[f, count], rsem, device))
            count += 1

        for i, step in enumerate(sides):
            for sub in (s, o):
                add(
                    copies,
                    packed_send.at[f],
                    packed_recv.at[f, i, s],
                    packed_rsem.at[f, i, s],
                    at(blk=blk_at(step), sub=sub),
                )
                add(
                    edges,
                    strip_send.at[f, edge_place],
                    corner_recv.at[f, i, o],
                    corner_rsem.at[f, i, o],
                    at(tube=behind, blk=blk_at(step), sub=sub),
                )
        for sub in (s, o):
            add(
                edges,
                main_send.at[f, edge_place],
                edge_recv.at[f, o],
                edge_rsem.at[f, o],
                at(tube=behind, sub=sub),
            )
        add(copies, main_send.at[f, own_place], main_recv.at[f], main_rsem.at[f], at(sub=o))
        @pl.when(has_behind)
        def _():
            for copy in edges:
                copy.start()

        packed = jnp.zeros((group, block), F32)
        start = pl.multiple_of(o * HALO, HALO)
        for g in range(PACK):
            packed = packed + pltpu.roll(
                strip_send[f, pl.ds(start + g * group, group), :], HALO + 2 * HALO * g, 1
            )
        packed_send[f] = packed
        for copy in copies:
            copy.start()
        return copies, edges

    def landed(buf, rsem):
        remote(buf, buf, rsem, rsem, at(sub=o)).wait_recv()

    def collect(f):
        other_rows = pl.ds(pl.multiple_of(o * (rows - inner), HALO), inner)
        total[f, edge_rows, :] = jnp.zeros((HALO, block), F32)
        total[f, pl.ds(pl.multiple_of(o * inner, HALO), rows - inner), :] = jnp.zeros(
            (rows - inner, block), F32
        )
        total[f, own_rows, :] = main_send[f, own_place, :]
        landed(main_recv.at[f], main_rsem.at[f])
        total[f, other_rows, :] += main_recv[f]
        for i in range(len(sides)):
            for sub in range(2):
                landed(packed_recv.at[f, i, sub], packed_rsem.at[f, i, sub])
                for g in range(PACK):
                    value = pltpu.roll(
                        packed_recv[f, i, sub], block - (HALO + 2 * HALO * g) % block, 1
                    )
                    start = sub * (rows - inner) + g * group
                    total[f, start : start + group, :] += jnp.where(lanes_of[i], value, 0.0)
        for n, (cond, start) in enumerate(((t > 0, 0), (t < tubes - 1, rows - HALO))):

            @pl.when(cond)
            def _():
                landed(edge_recv.at[f, n], edge_rsem.at[f, n])
                value = edge_recv[f, n]
                for i in range(len(sides)):
                    landed(corner_recv.at[f, i, n], corner_rsem.at[f, i, n])
                    value = value + jnp.where(lanes_of[i], corner_recv[f, i, n], 0.0)
                total[f, start : start + HALO, :] += value

    spread_d = adjoint(None)

    for copy in side_copies:
        copy.wait_recv()

    @pl.when(has_behind)
    def _():
        for copy in edge_copies:
            copy.wait_recv()

    @pl.when(jnp.logical_not(has_behind))
    def _():
        view[edge_place, :] = jnp.zeros((HALO, block), BF16)
        for i in range(len(sides)):
            side_view[i, edge_place, :] = jnp.zeros((HALO, block), BF16)

    if blks == 2:
        beside = side_view[0]
    else:
        beside = jnp.where(lane < block // 2, side_view[1], side_view[0])
    seen = jnp.concatenate([view[...], beside], axis=1)
    seen = jnp.concatenate([seen, jnp.zeros((2 * block - ext, 2 * block), BF16)], axis=0)
    blurred = jnp.zeros((half, block), F32)
    for n in range(2 * kernels):
        along = dot(row_band[n], seen).astype(BF16)
        both = lax.dot_general(
            along, col_band[n], (((1,), (1,)), ((), ())), preferred_element_type=F32
        )
        blurred = blurred + scaled[n] * both
    inverse = 1.0 / blurred

    coverage = gain_send[t]
    for j, copy in enumerate(gain_copies):
        copy.wait()
        coverage = coverage + gain_recv[j]
    sent_d = exchange(0, spread_d * coverage[0:1, 0:1])

    for copy in count_copies:
        copy.wait()
    counts = count_send[t].astype(F32)
    for j in range(tubes - 1):
        counts = counts + count_recv[j].astype(F32)
    sent_n = exchange(1, adjoint(counts * inverse))
    collect(0)
    collect(1)
    out_ref[...] = latent_ref[...] * total[1] / jnp.maximum(total[0], 0.25)

    for copy in side_copies:
        copy.wait_send()

    @pl.when(has_ahead)
    def _():
        for copy in edge_copies:
            copy.wait_send()

    for copies, edges in (sent_d, sent_n):
        for copy in copies:
            copy.wait_send()

        @pl.when(has_behind)
        def _():
            for copy in edges:
                copy.wait_send()


def body(tubes, blks, latent, weight_maps, row_taps, col_taps, exposures, gains, owners, offsets):
    rows, block = latent.shape
    half = rows // 2
    ext = half + 2 * HALO
    inner = half + HALO
    kernels = weight_maps.shape[0]
    slots = exposures.shape[1]
    nside = 1 if blks == 2 else 2
    peers = tubes - 1
    vmem = pl.BlockSpec(memory_space=pltpu.VMEM)
    anywhere = pl.BlockSpec(memory_space=pl.ANY)
    taps = row_taps.shape[1]
    dma = pltpu.SemaphoreType.DMA
    return pl.pallas_call(
        functools.partial(kernel, tubes, blks),
        out_shape=jax.ShapeDtypeStruct((rows, block), F32),
        in_specs=[anywhere] * 8,
        out_specs=vmem,
        scratch_shapes=[
            pltpu.VMEM((slots, block, block), BF16),
            pltpu.VMEM((rows, block), F32),
            pltpu.VMEM((kernels, half, block), BF16),
            pltpu.VMEM((kernels, taps), F32),
            pltpu.VMEM((kernels, taps), F32),
            pltpu.VMEM((1, slots), BF16),
            pltpu.VMEM((1, slots), jnp.int32),
            pltpu.VMEM((1, slots), jnp.int32),
            pltpu.VMEM((rows, block), BF16),
            pltpu.VMEM((ext, block), BF16),
            pltpu.VMEM((nside, ext, block), BF16),
            pltpu.VMEM((kernels, half, block), BF16),
            pltpu.VMEM((2 * kernels, 2 * block), F32),
            pltpu.VMEM((2 * kernels, 2 * block), F32),
            pltpu.VMEM((tubes, 8, block), F32),
            pltpu.VMEM((peers, 8, block), F32),
            pltpu.VMEM((tubes * TILE, slots * TILE), BF16),
            pltpu.VMEM((tubes, half, block), BF16),
            pltpu.VMEM((peers, half, block), BF16),
            pltpu.VMEM((2 * kernels, half, 2 * block), BF16),
            pltpu.VMEM((ext, 2 * kernels * half), BF16),
            pltpu.VMEM((2 * kernels, block, 2 * block), BF16),
            pltpu.VMEM((2 * kernels, half, block), F32),
            pltpu.VMEM((2 * kernels * half, 2 * block), BF16),
            pltpu.VMEM((2, ext, block), F32),
            pltpu.VMEM((2, ext, block), F32),
            pltpu.VMEM((2, inner // PACK, block), F32),
            pltpu.VMEM((2, inner, block), F32),
            pltpu.VMEM((2, 2, HALO, block), F32),
            pltpu.VMEM((2, nside, 2, inner // PACK, block), F32),
            pltpu.VMEM((2, nside, 2, HALO, block), F32),
            pltpu.VMEM((2, rows, block), F32),
            dma((PIECES,)),
            dma((7,)),
            dma((1 + 2 * nside,)),
            dma((1 + 2 * nside,)),
            dma((2,)),
            dma((2,)),
            dma((peers,)),
            dma((peers,)),
            dma((PIECES, peers)),
            dma((PIECES, peers)),
            dma((2, 4 * nside + 3)),
            dma((2,)),
            dma((2, 2)),
            dma((2, nside, 2)),
            dma((2, nside, 2)),
        ],
        compiler_params=pltpu.CompilerParams(
            collective_id=0, has_side_effects=True, vmem_limit_bytes=60 * 1024 * 1024
        ),
    )(latent, weight_maps, row_taps, col_taps, exposures[0], gains, owners.reshape(1, slots), offsets)


def solution(mesh):
    in_specs = (
        P(("sec", "tube"), "blk"),
        P("sub", ("sec", "tube"), "blk"),
        P("sub", None),
        P("sub", None),
        P("blk", ("sec", "tube"), None, None),
        P("blk", ("sec", "tube")),
        P("blk", ("sec", "tube"), None),
        P("blk", ("sec", "tube")),
    )
    out_specs = P(("sec", "tube"), "blk")
    run = functools.partial(body, mesh.shape["tube"], mesh.shape["blk"])
    return jax.shard_map(run, mesh=mesh, in_specs=in_specs, out_specs=out_specs, check_vma=False)
```
